32 devices in a mesh: groups: 2 (over y), seg: 4 (over z), ctx: 2 (over x), head: 2 (over core).
Axes of the slice: x: 2, y: 2, z: 4, core: 2. Of those that a mesh axis runs over, the one named last changes fastest.
Arguments:
- queries: bfloat16 [1024, 1024], P(('groups', 'ctx'), 'head'), parts along dimension 0, may hold values from -40 to 40
- cached_keys: bfloat16 [4096, 128], P(('groups', 'seg', 'ctx')), parts along dimension 0, may hold values from -20 to 20
- cached_values: bfloat16 [4096, 128], P(('groups', 'seg', 'ctx')), parts along dimension 0, may hold values from -6 to 6
- key_offsets: int32 [16], P('groups'), parts along dimension 0, may hold values from 0 to 1792, as said below
- vertical_blocks: int32 [16, 16], P('groups'), parts along dimension 0, may hold values from 0 to 31
- slash_offsets: int32 [16, 32], P('groups'), parts along dimension 0, may hold values from 0 to 24, as said below
Outputs:
- attended: bfloat16 [1024, 1024], P(('groups', 'ctx'), 'head'), parts along dimension 0
The draws below stay inside these ranges and needn't reach their ends.
There are 2 independent parts, one for each index of `groups`. The reference program is written for one: setup_inputs(seed, part) draws one part's arguments, and reference() takes and returns one part's arrays. A program takes and returns all parts, laid end to end along the dimension named above; each array names one. Nothing has to cross between parts.
Inputs may be any that keep to these rules, and one draw needn't show every extreme that they name: `key_offsets`: holds k * 256 for every k below the number of key shards, each once. `slash_offsets`: column 0 is 0 in every row.
All inputs are finite; a program needn't handle non-finite values.
Results may differ from the reference program's by a relative error of at most 0.028.
Values may be sent and summed in bfloat16 or wider, within the bound.
A program may use at most 64 MiB of HBM per device.

```python
import math
import jax
import jax.numpy as jnp
from jax import lax

HEAD_DIM = 128
QUERY_HEADS = 8
BLOCK = 64
VERTICAL = 16
SLASHES = 32
QUERY_ROWS = 256
KEY_ROWS = 256
KEY_TOTAL = 2048
PREFIX = 1536
QUERY_BLOCKS = 8
KEY_BLOCKS = 32
N_SEG = 4
N_CTX = 2


def slow_columns(columns):
    within = jnp.arange(columns, dtype=jnp.int32) % HEAD_DIM
    half_width = HEAD_DIM // 2
    return within % half_width >= half_width - HEAD_DIM // 8


def changed_column(columns):
    within = jnp.arange(columns, dtype=jnp.int32) % HEAD_DIM
    return within == HEAD_DIM // 2 - 1


def strong_rows(key):
    total_rows = QUERY_ROWS * N_CTX
    pick_key, sign_key, query_key, cache_key, tie_key = jax.random.split(jax.random.fold_in(key, 17), 5)
    index = jnp.arange(total_rows, dtype=jnp.int32)
    forced_high = index == 1
    forced_low = index == total_rows - 1
    picked = (jax.random.randint(pick_key, (total_rows,), 0, 32, dtype=jnp.int32) == 0) | forced_high | forced_low
    picked = picked & (index % 2 == 1)
    signs = jnp.where(jax.random.bernoulli(sign_key, 0.5, (total_rows, HEAD_DIM)), 1.0, -1.0).astype(jnp.float32)
    query_size = jax.random.uniform(query_key, (total_rows,), jnp.float32, 8.0, 38.0)
    cache_size = jax.random.uniform(cache_key, (total_rows,), jnp.float32, 4.0, 19.0)
    query_size = jnp.where(forced_high | forced_low, 30.0, query_size)
    cache_size = jnp.where(forced_high, 18.0, jnp.where(forced_low, 4.0, cache_size))
    tie_gap = jax.random.uniform(tie_key, (total_rows,), jnp.float32, 1.5, 2.5)
    return (picked, signs, query_size, cache_size, tie_gap)


def draw_queries(key, part):
    first_key = jax.random.fold_in(jax.random.fold_in(key, 11), 0)
    total_rows = QUERY_ROWS * N_CTX
    columns = QUERY_HEADS * HEAD_DIM
    drawn = jnp.clip(jax.random.normal(first_key, (total_rows, columns), jnp.float32), -6.0, 6.0)
    picked, signs, query_size, cache_size, tie_gap = strong_rows(key)
    strong_entries = jnp.tile(signs, (1, QUERY_HEADS)) * query_size[:, None]
    strong_entries = jnp.where(slow_columns(columns)[None, :], strong_entries, 0.0)
    values = jnp.where(picked[:, None], strong_entries, drawn)
    return values.astype(jnp.bfloat16)


def draw_cached_keys(key, part):
    first_key = jax.random.fold_in(jax.random.fold_in(key, 13), 0)
    total_rows = KEY_ROWS * N_SEG * N_CTX
    query_total = QUERY_ROWS * N_CTX
    drawn = jnp.clip(jax.random.normal(first_key, (total_rows, HEAD_DIM), jnp.float32), -6.0, 6.0)
    picked, signs, query_size, cache_size, tie_gap = strong_rows(key)
    offsets = draw_key_offsets(key, part)
    rows = jnp.arange(total_rows, dtype=jnp.int32)
    positions = offsets[rows // KEY_ROWS] + rows % KEY_ROWS
    query_index = (positions - PREFIX).astype(jnp.int32)
    next_index = (query_index + 1).astype(jnp.int32)
    own_clipped = jnp.clip(query_index, 0, query_total - 1).astype(jnp.int32)
    next_clipped = jnp.clip(next_index, 0, query_total - 1).astype(jnp.int32)
    self_hit = (query_index >= 0) & picked[own_clipped]
    prev_hit = (next_index >= 0) & (next_index < query_total) & picked[next_clipped]
    source = jnp.where(self_hit, own_clipped, next_clipped).astype(jnp.int32)
    change = tie_gap[source] * math.sqrt(HEAD_DIM) / query_size[source]
    lowered = jnp.where(prev_hit[:, None] & changed_column(HEAD_DIM)[None, :], change[:, None], 0.0)
    strong_entries = signs[source] * (cache_size[source][:, None] - lowered)
    use_strong = (self_hit | prev_hit)[:, None] & slow_columns(HEAD_DIM)[None, :]
    values = jnp.where(use_strong, strong_entries, drawn)
    return values.astype(jnp.bfloat16)


def draw_key_offsets(key, part):
    return (jax.random.permutation(key, N_SEG * N_CTX) * KEY_ROWS).astype(jnp.int32)


def draw_slash_offsets(key, part):
    drawn_offsets = jax.random.randint(key, (QUERY_BLOCKS, SLASHES), 1, PREFIX // BLOCK + 1, dtype=jnp.int32)
    column = jnp.arange(SLASHES, dtype=jnp.int32)[None, :]
    row_index = jnp.arange(QUERY_BLOCKS, dtype=jnp.int32)[:, None]
    drawn_offsets = jnp.where(column == 0, 0, drawn_offsets)
    drawn_offsets = jnp.where((row_index == 0) & (column == 1), PREFIX // BLOCK, drawn_offsets)
    return drawn_offsets.astype(jnp.int32)


def set_ends(entries, rng, least, largest):
    spot = [jax.random.randint(jax.random.fold_in(rng, axis), (), 0, length) for axis, length in enumerate(entries.shape)]
    longest = entries.shape.index(max(entries.shape))
    beside = spot[:longest] + [(spot[longest] + 1) % entries.shape[longest]] + spot[longest + 1:]
    return entries.at[tuple(spot)].set(least).at[tuple(beside)].set(largest)


def level_of(rng, shape, shards, least, high):
    def one(position, blocks):
        heights = jax.random.uniform(jax.random.fold_in(jax.random.fold_in(rng, 6), position), (blocks,), jnp.float32, least / len(shards), high / len(shards))
        return jnp.repeat(jnp.exp(heights), shape[position] // blocks).reshape((-1,) + (1,) * (len(shape) - position - 1))

    loudness = one(*shards[0])
    for cut in shards[1:]:
        loudness = loudness * one(*cut)
    return loudness


def noise(stream_key, dims, width, most, shards=(), held_as=jnp.bfloat16):
    entries = width * jax.random.normal(stream_key, dims, jnp.float32)
    if shards:
        entries = entries * level_of(stream_key, dims, shards, -0.22, 0.18)
    return jnp.clip(entries, -most, most).astype(held_as)


def setup_inputs(seed: int = 0, part: int = 0) -> dict:
    key_of = jax.random.split(jax.random.key(seed), 7)
    part_keys = jax.random.split(jax.random.fold_in(key_of[6], part), 7)
    return {
        "queries": draw_queries(jax.random.fold_in(jax.random.fold_in(key_of[6], part), 71), part),
        "cached_keys": draw_cached_keys(jax.random.fold_in(jax.random.fold_in(key_of[6], part), 71), part),
        "cached_values": noise(part_keys[2], (KEY_TOTAL, HEAD_DIM), 1.0, 6.0, ((0, 8),)),
        "key_offsets": draw_key_offsets(jax.random.fold_in(jax.random.fold_in(key_of[6], part), 71), part),
        "vertical_blocks": set_ends(jax.random.randint(part_keys[4], (QUERY_BLOCKS, VERTICAL), 0, KEY_BLOCKS), jax.random.fold_in(part_keys[4], 1), 0, KEY_BLOCKS - 1).astype(jnp.int32),
        "slash_offsets": draw_slash_offsets(jax.random.fold_in(jax.random.fold_in(key_of[6], part), 71), part),
    }


ROPE_THETA = 500000.0
ROPE_FACTOR = 8.0
LOW_FACTOR = 1.0
HIGH_FACTOR = 4.0
TRAINED_CONTEXT = 8192.0
MASKED_SCORE = -1.0e30


def inverse_frequencies(vector_width):
    exponent = jnp.arange(0, vector_width, 2, dtype=jnp.float32) / vector_width
    base_frequency = 1.0 / (ROPE_THETA ** exponent)
    wavelength = 2.0 * math.pi / base_frequency
    smooth = (TRAINED_CONTEXT / wavelength - LOW_FACTOR) / (HIGH_FACTOR - LOW_FACTOR)
    blended = (1.0 - smooth) * base_frequency / ROPE_FACTOR + smooth * base_frequency
    return jnp.where(wavelength < TRAINED_CONTEXT / HIGH_FACTOR, base_frequency,
                     jnp.where(wavelength > TRAINED_CONTEXT / LOW_FACTOR, base_frequency / ROPE_FACTOR, blended))


def rotate(vectors, positions):
    vector_width = vectors.shape[-1]
    half_width = vector_width // 2
    angles = positions.astype(jnp.float32)[:, None] * inverse_frequencies(vector_width)[None, :]
    cosine = jnp.concatenate([jnp.cos(angles), jnp.cos(angles)], axis=-1)[:, None, :]
    sine_table = jnp.concatenate([jnp.sin(angles), jnp.sin(angles)], axis=-1)[:, None, :]
    widened = vectors.astype(jnp.float32)
    turned = jnp.concatenate([-widened[..., half_width:], widened[..., :half_width]], axis=-1)
    return (widened * cosine + turned * sine_table).astype(jnp.bfloat16)


def widen(rounded):
    return lax.optimization_barrier(rounded).astype(jnp.float32)


def reference(queries, cached_keys, cached_values, key_offsets, vertical_blocks, slash_offsets):
    total_queries = queries.shape[0]
    total_keys = cached_keys.shape[0]
    prefix = total_keys - total_queries
    query_positions = (prefix + jnp.arange(total_queries, dtype=jnp.int32)).astype(jnp.int32)
    key_positions = (key_offsets[:, None] + jnp.arange(KEY_ROWS, dtype=jnp.int32)[None, :]).reshape(-1)
    rotated_queries = rotate(queries.reshape(total_queries, QUERY_HEADS, HEAD_DIM), query_positions)
    rotated_keys = widen(rotate(cached_keys.reshape(total_keys, 1, HEAD_DIM), key_positions).reshape(total_keys, HEAD_DIM))
    value_rows = cached_values.astype(jnp.float32)
    block_ids = jnp.arange(total_keys // BLOCK, dtype=jnp.int32)
    key_block = key_positions // BLOCK
    row_tile = math.gcd(total_queries, 128)
    score_scale = HEAD_DIM ** -0.5

    def attend_rows(tile_number):
        first_row = (tile_number * row_tile).astype(jnp.int32)
        query_tile = widen(lax.dynamic_slice_in_dim(rotated_queries, first_row, row_tile, 0))
        positions = lax.dynamic_slice_in_dim(query_positions, first_row, row_tile, 0)
        list_rows = (positions - prefix) // BLOCK
        vertical_hit = jnp.any(vertical_blocks[list_rows][:, :, None] == block_ids[None, None, :], axis=1)
        distance = positions[:, None] // BLOCK - block_ids[None, :]
        slash_hit = jnp.any(slash_offsets[list_rows][:, :, None] == distance[:, None, :], axis=1)
        allowed = (vertical_hit | slash_hit)[:, key_block] & (key_positions[None, :] <= positions[:, None])
        scores = jnp.einsum("thd,kd->thk", query_tile, rotated_keys, precision=lax.Precision.HIGHEST) * score_scale
        scores = jnp.where(allowed[:, None, :], scores, MASKED_SCORE)
        row_peak = jnp.max(scores, axis=-1, keepdims=True)
        weights = jnp.where(allowed[:, None, :], jnp.exp(scores - row_peak), 0.0)
        denominator = jnp.sum(weights, axis=-1)
        rounded_weights = widen(weights.astype(jnp.bfloat16))
        numerator = jnp.einsum("thk,kd->thd", rounded_weights, value_rows, precision=lax.Precision.HIGHEST)
        return (numerator / denominator[..., None]).astype(jnp.bfloat16).reshape(row_tile, QUERY_HEADS * HEAD_DIM)

    attended = lax.map(attend_rows, jnp.arange(total_queries // row_tile, dtype=jnp.int32))
    return attended.reshape(total_queries, QUERY_HEADS * HEAD_DIM)
```

```python
import functools
import math

import jax
import jax.numpy as jnp
import numpy as np
from jax import lax
from jax.experimental import pallas as pl
from jax.experimental.pallas import tpu as pltpu
from jax.sharding import PartitionSpec as P

HEAD_DIM = 128
BLOCK = 64
ROPE_THETA = 500000.0
ROPE_FACTOR = 8.0
LOW_FACTOR = 1.0
HIGH_FACTOR = 4.0
TRAINED_CONTEXT = 8192.0
MASKED = -1e30
EXP2_SCALE = HEAD_DIM ** -0.5 * math.log2(math.e)
MESH = pl.DeviceIdType.MESH


def rope_tables(positions):
    half = HEAD_DIM // 2
    base = ROPE_THETA ** -(np.arange(half, dtype=np.float64) * 2.0 / HEAD_DIM)
    wavelength = 2.0 * np.pi / base
    smooth = (TRAINED_CONTEXT / wavelength - LOW_FACTOR) / (HIGH_FACTOR - LOW_FACTOR)
    blended = (1.0 - smooth) * base / ROPE_FACTOR + smooth * base
    frequency = np.where(
        wavelength < TRAINED_CONTEXT / HIGH_FACTOR,
        base,
        np.where(wavelength > TRAINED_CONTEXT / LOW_FACTOR, base / ROPE_FACTOR, blended),
    )
    angles = positions.astype(np.float64)[:, None] * frequency[None, :]
    cosine = np.concatenate([np.cos(angles), np.cos(angles)], axis=1)
    sine = np.concatenate([-np.sin(angles), np.sin(angles)], axis=1)
    return cosine.astype(np.float32), sine.astype(np.float32)


def flip(index, step, size):
    result, bit = 0, 1
    while bit < size:
        result = result + ((index // bit) % 2 + (step // bit) % 2) % 2 * bit
        bit *= 2
    return result


def kernel(
    n_seg, n_ctx,
    offsets_ref, q_ref, k_ref, v_ref, vert_ref, slash_ref, cos_ref, sin_ref, ocos_ref, osin_ref,
    out_ref,
    kv, qt, bias_tab, peak, total, numer,
    send_z, send_x, send_sib, recv,
):
    seg, ctx, head = lax.axis_index("seg"), lax.axis_index("ctx"), lax.axis_index("head")
    rows, heads = q_ref.shape[0], q_ref.shape[1] // HEAD_DIM
    keys = k_ref.shape[0]
    prefix = keys * n_seg * n_ctx - rows * n_ctx
    other = 1 - head
    own = seg * n_ctx + ctx

    def shard(t, u):
        return flip(seg, t, n_seg) * n_ctx + flip(ctx, u, n_ctx)

    barrier = pltpu.get_barrier_semaphore()
    for t in range(1, n_seg):
        pl.semaphore_signal(
            barrier, inc=1, device_id={"seg": flip(seg, t, n_seg)}, device_id_type=MESH
        )
    for u in range(1, n_ctx):
        pl.semaphore_signal(
            barrier, inc=1, device_id={"ctx": flip(ctx, u, n_ctx)}, device_id_type=MESH
        )
    pl.semaphore_signal(barrier, inc=1, device_id={"head": other}, device_id_type=MESH)

    def rotation(index):
        ocos = ocos_ref[pl.ds(index, 1), :]
        osin = osin_ref[pl.ds(index, 1), :]
        cosine = ocos * cos_ref[...] - osin * sin_ref[...]
        sine = osin * cos_ref[...] + ocos * sin_ref[...]
        return cosine, sine

    def rotate(x, cosine, sine):
        x = x.astype(jnp.float32)
        return x * cosine + pltpu.roll(x, HEAD_DIM // 2, 1) * sine

    cosine, sine = rotation(offsets_ref[own] // keys)
    kv[0, own] = rotate(k_ref[...], cosine, sine).astype(jnp.bfloat16)
    kv[1, own] = v_ref[...]

    pl.semaphore_wait(barrier, n_seg + n_ctx - 1)

    def copy_z(t):
        return pltpu.make_async_remote_copy(
            src_ref=kv.at[head, own], dst_ref=kv.at[head, own],
            send_sem=send_z.at[t], recv_sem=recv.at[head, own],
            device_id={"seg": flip(seg, t, n_seg)}, device_id_type=MESH,
        )

    def copy_x(t, u):
        index = shard(t, 0)
        return pltpu.make_async_remote_copy(
            src_ref=kv.at[head, index], dst_ref=kv.at[head, index],
            send_sem=send_x.at[t, u], recv_sem=recv.at[head, index],
            device_id={"ctx": flip(ctx, u, n_ctx)}, device_id_type=MESH,
        )

    def copy_sib(t, u):
        index = shard(t, u)
        return pltpu.make_async_remote_copy(
            src_ref=kv.at[head, index], dst_ref=kv.at[head, index],
            send_sem=send_sib.at[t, u], recv_sem=recv.at[head, index],
            device_id={"head": other}, device_id_type=MESH,
        )

    def arrived(kind, index):
        pltpu.make_async_remote_copy(
            src_ref=kv.at[kind, index], dst_ref=kv.at[kind, index],
            send_sem=send_z.at[0], recv_sem=recv.at[kind, index],
            device_id={"head": other}, device_id_type=MESH,
        ).wait_recv()

    for u in range(1, n_ctx):
        copy_x(0, u).start()
    for t in range(1, n_seg):
        copy_z(t).start()

    cosine, sine = rotation((prefix + ctx * rows) // keys)
    for h in range(heads):
        x = q_ref[:, h * HEAD_DIM : (h + 1) * HEAD_DIM]
        qt[:, h * rows : (h + 1) * rows] = rotate(x, cosine, sine).T.astype(jnp.bfloat16)

    lists, blocks = vert_ref.shape[0], bias_tab.shape[0]
    block_id = lax.broadcasted_iota(jnp.int32, (lists, blocks), 1)
    from_slash = (
        prefix // BLOCK + lax.broadcasted_iota(jnp.int32, slash_ref.shape, 0) - slash_ref[...]
    )
    vertical = vert_ref[...]
    hit = vertical[:, 0:1] == block_id
    for i in range(1, vertical.shape[1]):
        hit = hit | (vertical[:, i : i + 1] == block_id)
    for i in range(from_slash.shape[1]):
        hit = hit | (from_slash[:, i : i + 1] == block_id)
    list_id = lax.broadcasted_iota(jnp.int32, (lists, rows), 0)
    token_list = ctx * (rows // BLOCK) + lax.broadcasted_iota(jnp.int32, (lists, rows), 1) // BLOCK
    pick = jnp.where(list_id == token_list, 1.0, 0.0)
    spread = lax.dot_general(
        jnp.where(hit, 1.0, 0.0).T, pick, (((1,), (0,)), ((), ())),
        preferred_element_type=jnp.float32,
    )
    bias_tab[...] = jnp.where(spread > 0.5, 0.0, MASKED)

    lead = (
        prefix + ctx * rows
        + lax.broadcasted_iota(jnp.int32, (BLOCK, rows), 1)
        - lax.broadcasted_iota(jnp.int32, (BLOCK, rows), 0)
    )

    def attend(index, first=False):
        offset = offsets_ref[index]
        pieces = []
        for i in range(keys // BLOCK):
            row = bias_tab[pl.ds(offset // BLOCK + i, 1), :]
            pieces.append(jnp.where(lead >= offset + i * BLOCK, row, MASKED))
        bias = jnp.concatenate(pieces, axis=0)
        key_tile = kv[0, index]
        value_tile = kv[1, index].T
        for h in range(heads):
            columns = slice(h * rows, (h + 1) * rows)
            scores = (
                jnp.dot(key_tile, qt[:, columns], preferred_element_type=jnp.float32) + bias
            )
            fresh = jnp.max(scores, axis=0, keepdims=True)
            if not first:
                old = peak[:, columns]
                fresh = jnp.maximum(old, fresh)
            weights = jnp.exp2((scores - fresh) * EXP2_SCALE)
            added = jnp.sum(weights, axis=0, keepdims=True)
            product = jnp.dot(
                value_tile, weights.astype(jnp.bfloat16), preferred_element_type=jnp.float32
            )
            if not first:
                rescale = jnp.exp2((old - fresh) * EXP2_SCALE)
                added = added + total[:, columns] * rescale
                product = product + numer[:, columns] * rescale
            peak[:, columns] = fresh
            total[:, columns] = added
            numer[:, columns] = product

    attend(own, True)

    def across(t):
        for u in range(1, n_ctx):
            arrived(head, shard(t, u))
            copy_sib(t, u).start()

    def attend_across(t):
        for u in range(1, n_ctx):
            arrived(other, shard(t, u))
            attend(shard(t, u))

    def step(t, carry):
        arrived(head, shard(t, 0))
        for u in range(1, n_ctx):
            copy_x(t, u).start()
        copy_sib(t, 0).start()
        across(t - 1)
        attend_across(t - 1)
        arrived(other, shard(t, 0))
        attend(shard(t, 0))
        return carry

    lax.fori_loop(1, n_seg, step, 0)
    across(n_seg - 1)
    attend_across(n_seg - 1)

    for h in range(heads):
        columns = slice(h * rows, (h + 1) * rows)
        out_ref[:, h * HEAD_DIM : (h + 1) * HEAD_DIM] = (
            (numer[:, columns] / total[:, columns]).T.astype(jnp.bfloat16)
        )

    for t in range(1, n_seg):
        copy_z(t).wait_send()
        copy_sib(t, 0).wait_send()
    for t in range(n_seg):
        for u in range(1, n_ctx):
            copy_x(t, u).wait_send()
            copy_sib(t, u).wait_send()


def solution(mesh):
    n_seg, n_ctx = mesh.shape["seg"], mesh.shape["ctx"]

    def local(queries, cached_keys, cached_values, key_offsets, vertical_blocks, slash_offsets):
        rows, columns = queries.shape
        heads = columns // HEAD_DIM
        keys = cached_keys.shape[0]
        shards = n_seg * n_ctx
        blocks = -(-(keys * shards // BLOCK) // 128) * 128
        cosine, sine = rope_tables(np.arange(keys))
        ocos, osin = rope_tables(np.arange(shards) * keys)
        vmem = pl.BlockSpec(memory_space=pltpu.VMEM)
        smem = pl.BlockSpec(memory_space=pltpu.SMEM)
        return pl.pallas_call(
            functools.partial(kernel, n_seg, n_ctx),
            out_shape=jax.ShapeDtypeStruct((rows, columns), jnp.bfloat16),
            in_specs=[smem] + [vmem] * 9,
            out_specs=vmem,
            scratch_shapes=[
                pltpu.VMEM((2, shards, keys, HEAD_DIM), jnp.bfloat16),
                pltpu.VMEM((HEAD_DIM, heads * rows), jnp.bfloat16),
                pltpu.VMEM((blocks, rows), jnp.float32),
                pltpu.VMEM((1, heads * rows), jnp.float32),
                pltpu.VMEM((1, heads * rows), jnp.float32),
                pltpu.VMEM((HEAD_DIM, heads * rows), jnp.float32),
                pltpu.SemaphoreType.DMA((n_seg,)),
                pltpu.SemaphoreType.DMA((n_seg, n_ctx)),
                pltpu.SemaphoreType.DMA((n_seg, n_ctx)),
                pltpu.SemaphoreType.DMA((2, shards)),
            ],
            compiler_params=pltpu.CompilerParams(
                collective_id=0, has_side_effects=True, vmem_limit_bytes=48 * 1024 * 1024
            ),
        )(
            key_offsets, queries, cached_keys, cached_values, vertical_blocks, slash_offsets,
            cosine, sine, ocos, osin,
        )

    return jax.shard_map(
        local,
        mesh=mesh,
        in_specs=(
            P(("groups", "ctx"), "head"),
            P(("groups", "seg", "ctx"), None),
            P(("groups", "seg", "ctx"), None),
            P("groups"),
            P("groups", None),
            P("groups", None),
        ),
        out_specs=P(("groups", "ctx"), "head"),
        check_vma=False,
    )
```

```python
import functools
import math

import jax
import jax.numpy as jnp
import numpy as np
from jax import lax
from jax.experimental import pallas as pl
from jax.experimental.pallas import tpu as pltpu
from jax.sharding import PartitionSpec as P

HEAD_DIM = 128
BLOCK = 64
ROPE_THETA = 500000.0
ROPE_FACTOR = 8.0
LOW_FACTOR = 1.0
HIGH_FACTOR = 4.0
TRAINED_CONTEXT = 8192.0
MASKED = -1e30
EXP2_SCALE = HEAD_DIM ** -0.5 * math.log2(math.e)
MESH = pl.DeviceIdType.MESH


def rope_tables(positions):
    half = HEAD_DIM // 2
    base = ROPE_THETA ** -(np.arange(half, dtype=np.float64) * 2.0 / HEAD_DIM)
    wavelength = 2.0 * np.pi / base
    smooth = (TRAINED_CONTEXT / wavelength - LOW_FACTOR) / (HIGH_FACTOR - LOW_FACTOR)
    blended = (1.0 - smooth) * base / ROPE_FACTOR + smooth * base
    frequency = np.where(
        wavelength < TRAINED_CONTEXT / HIGH_FACTOR,
        base,
        np.where(wavelength > TRAINED_CONTEXT / LOW_FACTOR, base / ROPE_FACTOR, blended),
    )
    angles = positions.astype(np.float64)[:, None] * frequency[None, :]
    cosine = np.concatenate([np.cos(angles), np.cos(angles)], axis=1)
    sine = np.concatenate([-np.sin(angles), np.sin(angles)], axis=1)
    return cosine.astype(np.float32), sine.astype(np.float32)


def flip(index, step, size):
    result, bit = 0, 1
    while bit < size:
        result = result + ((index // bit) % 2 + (step // bit) % 2) % 2 * bit
        bit *= 2
    return result


def kernel(
    n_seg, n_ctx,
    offsets_hbm, q_hbm, k_hbm, v_hbm, vert_hbm, slash_hbm, table_hbm, start_hbm,
    out_ref,
    offsets_ref, q_ref, k_ref, vert_ref, slash_ref, table_ref, start_ref,
    kv, qt, bias_tab, peak, total, numer,
    load, send_z, send_x, send_sib, recv,
):
    seg, ctx, head = lax.axis_index("seg"), lax.axis_index("ctx"), lax.axis_index("head")
    rows, heads = q_ref.shape[0], q_ref.shape[1] // HEAD_DIM
    keys = k_ref.shape[0]
    prefix = keys * n_seg * n_ctx - rows * n_ctx
    other = 1 - head
    own = seg * n_ctx + ctx

    def shard(t, u):
        return flip(seg, t, n_seg) * n_ctx + flip(ctx, u, n_ctx)

    loads = [
        pltpu.make_async_copy(source, target, load.at[i])
        for i, (source, target) in enumerate((
            (offsets_hbm, offsets_ref),
            (start_hbm, start_ref),
            (k_hbm, k_ref),
            (table_hbm, table_ref),
            (v_hbm, kv.at[1, own]),
            (q_hbm, q_ref),
            (vert_hbm, vert_ref),
            (slash_hbm, slash_ref),
        ))
    ]
    for copy in loads:
        copy.start()

    barrier = pltpu.get_barrier_semaphore()
    for t in range(1, n_seg):
        pl.semaphore_signal(
            barrier, inc=1, device_id={"seg": flip(seg, t, n_seg)}, device_id_type=MESH
        )
    for u in range(1, n_ctx):
        pl.semaphore_signal(
            barrier, inc=1, device_id={"ctx": flip(ctx, u, n_ctx)}, device_id_type=MESH
        )
    pl.semaphore_signal(barrier, inc=1, device_id={"head": other}, device_id_type=MESH)

    def rotation(index):
        ocos = start_ref[0, pl.ds(index, 1), :]
        osin = start_ref[1, pl.ds(index, 1), :]
        cosine = ocos * table_ref[0] - osin * table_ref[1]
        sine = osin * table_ref[0] + ocos * table_ref[1]
        return cosine, sine

    def rotate(x, cosine, sine):
        x = x.astype(jnp.float32)
        return x * cosine + pltpu.roll(x, HEAD_DIM // 2, 1) * sine

    for copy in loads[:4]:
        copy.wait()
    cosine, sine = rotation(offsets_ref[own] // keys)
    kv[0, own] = rotate(k_ref[...], cosine, sine).astype(jnp.bfloat16)
    loads[4].wait()

    pl.semaphore_wait(barrier, n_seg + n_ctx - 1)

    def copy_z(t):
        return pltpu.make_async_remote_copy(
            src_ref=kv.at[head, own], dst_ref=kv.at[head, own],
            send_sem=send_z.at[t], recv_sem=recv.at[head, own],
            device_id={"seg": flip(seg, t, n_seg)}, device_id_type=MESH,
        )

    def copy_x(t, u):
        index = shard(t, 0)
        return pltpu.make_async_remote_copy(
            src_ref=kv.at[head, index], dst_ref=kv.at[head, index],
            send_sem=send_x.at[t, u], recv_sem=recv.at[head, index],
            device_id={"ctx": flip(ctx, u, n_ctx)}, device_id_type=MESH,
        )

    def copy_sib(t, u):
        index = shard(t, u)
        return pltpu.make_async_remote_copy(
            src_ref=kv.at[head, index], dst_ref=kv.at[head, index],
            send_sem=send_sib.at[t, u], recv_sem=recv.at[head, index],
            device_id={"head": other}, device_id_type=MESH,
        )

    def arrived(kind, index):
        pltpu.make_async_remote_copy(
            src_ref=kv.at[kind, index], dst_ref=kv.at[kind, index],
            send_sem=send_z.at[0], recv_sem=recv.at[kind, index],
            device_id={"head": other}, device_id_type=MESH,
        ).wait_recv()

    for u in range(1, n_ctx):
        copy_x(0, u).start()
    for t in range(1, n_seg):
        copy_z(t).start()

    for copy in loads[5:]:
        copy.wait()
    cosine, sine = rotation((prefix + ctx * rows) // keys)
    for h in range(heads):
        x = q_ref[:, h * HEAD_DIM : (h + 1) * HEAD_DIM]
        qt[:, h * rows : (h + 1) * rows] = rotate(x, cosine, sine).T.astype(jnp.bfloat16)

    lists, blocks = vert_ref.shape[0], bias_tab.shape[0]
    block_id = lax.broadcasted_iota(jnp.int32, (lists, blocks), 1)
    from_slash = (
        prefix // BLOCK + lax.broadcasted_iota(jnp.int32, slash_ref.shape, 0) - slash_ref[...]
    )
    vertical = vert_ref[...]
    hit = vertical[:, 0:1] == block_id
    for i in range(1, vertical.shape[1]):
        hit = hit | (vertical[:, i : i + 1] == block_id)
    for i in range(from_slash.shape[1]):
        hit = hit | (from_slash[:, i : i + 1] == block_id)
    list_id = lax.broadcasted_iota(jnp.int32, (lists, rows), 0)
    token_list = ctx * (rows // BLOCK) + lax.broadcasted_iota(jnp.int32, (lists, rows), 1) // BLOCK
    pick = jnp.where(list_id == token_list, 1.0, 0.0)
    spread = lax.dot_general(
        jnp.where(hit, 1.0, 0.0).T, pick, (((1,), (0,)), ((), ())),
        preferred_element_type=jnp.float32,
    )
    bias_tab[...] = jnp.where(spread > 0.5, 0.0, MASKED)

    lead = (
        prefix + ctx * rows
        + lax.broadcasted_iota(jnp.int32, (BLOCK, rows), 1)
        - lax.broadcasted_iota(jnp.int32, (BLOCK, rows), 0)
    )

    def attend(index, first=False):
        offset = offsets_ref[index]
        pieces = []
        for i in range(keys // BLOCK):
            row = bias_tab[pl.ds(offset // BLOCK + i, 1), :]
            pieces.append(jnp.where(lead >= offset + i * BLOCK, row, MASKED))
        bias = jnp.concatenate(pieces, axis=0)
        key_tile = kv[0, index]
        value_tile = kv[1, index].T
        for h in range(heads):
            columns = slice(h * rows, (h + 1) * rows)
            scores = (
                jnp.dot(key_tile, qt[:, columns], preferred_element_type=jnp.float32) + bias
            )
            fresh = jnp.max(scores, axis=0, keepdims=True)
            if not first:
                old = peak[:, columns]
                fresh = jnp.maximum(old, fresh)
            weights = jnp.exp2((scores - fresh) * EXP2_SCALE)
            added = jnp.sum(weights, axis=0, keepdims=True)
            product = jnp.dot(
                value_tile, weights.astype(jnp.bfloat16), preferred_element_type=jnp.float32
            )
            if not first:
                rescale = jnp.exp2((old - fresh) * EXP2_SCALE)
                added = added + total[:, columns] * rescale
                product = product + numer[:, columns] * rescale
            peak[:, columns] = fresh
            total[:, columns] = added
            numer[:, columns] = product

    attend(own, True)

    def across(t):
        for u in range(1, n_ctx):
            arrived(head, shard(t, u))
            copy_sib(t, u).start()

    def attend_across(t):
        for u in range(1, n_ctx):
            arrived(other, shard(t, u))
            attend(shard(t, u))

    def step(t, carry):
        arrived(head, shard(t, 0))
        for u in range(1, n_ctx):
            copy_x(t, u).start()
        copy_sib(t, 0).start()
        across(t - 1)
        attend_across(t - 1)
        arrived(other, shard(t, 0))
        attend(shard(t, 0))
        return carry

    lax.fori_loop(1, n_seg, step, 0)
    across(n_seg - 1)
    attend_across(n_seg - 1)

    for h in range(heads):
        columns = slice(h * rows, (h + 1) * rows)
        out_ref[:, h * HEAD_DIM : (h + 1) * HEAD_DIM] = (
            (numer[:, columns] / total[:, columns]).T.astype(jnp.bfloat16)
        )

    for t in range(1, n_seg):
        copy_z(t).wait_send()
        copy_sib(t, 0).wait_send()
    for t in range(n_seg):
        for u in range(1, n_ctx):
            copy_x(t, u).wait_send()
            copy_sib(t, u).wait_send()


def solution(mesh):
    n_seg, n_ctx = mesh.shape["seg"], mesh.shape["ctx"]

    def local(queries, cached_keys, cached_values, key_offsets, vertical_blocks, slash_offsets):
        rows, columns = queries.shape
        heads = columns // HEAD_DIM
        keys = cached_keys.shape[0]
        shards = n_seg * n_ctx
        blocks = -(-(keys * shards // BLOCK) // 128) * 128
        table = np.stack(rope_tables(np.arange(keys)))
        start = np.stack(rope_tables(np.arange(shards) * keys))
        operands = (
            key_offsets, queries, cached_keys, cached_values, vertical_blocks, slash_offsets,
            table, start,
        )
        return pl.pallas_call(
            functools.partial(kernel, n_seg, n_ctx),
            out_shape=jax.ShapeDtypeStruct((rows, columns), jnp.bfloat16),
            in_specs=[pl.BlockSpec(memory_space=pltpu.HBM)] * len(operands),
            out_specs=pl.BlockSpec(memory_space=pltpu.VMEM),
            scratch_shapes=[
                pltpu.SMEM(key_offsets.shape, jnp.int32),
                pltpu.VMEM(queries.shape, jnp.bfloat16),
                pltpu.VMEM(cached_keys.shape, jnp.bfloat16),
                pltpu.VMEM(vertical_blocks.shape, jnp.int32),
                pltpu.VMEM(slash_offsets.shape, jnp.int32),
                pltpu.VMEM(table.shape, jnp.float32),
                pltpu.VMEM(start.shape, jnp.float32),
                pltpu.VMEM((2, shards, keys, HEAD_DIM), jnp.bfloat16),
                pltpu.VMEM((HEAD_DIM, heads * rows), jnp.bfloat16),
                pltpu.VMEM((blocks, rows), jnp.float32),
                pltpu.VMEM((1, heads * rows), jnp.float32),
                pltpu.VMEM((1, heads * rows), jnp.float32),
                pltpu.VMEM((HEAD_DIM, heads * rows), jnp.float32),
                pltpu.SemaphoreType.DMA((len(operands),)),
                pltpu.SemaphoreType.DMA((n_seg,)),
                pltpu.SemaphoreType.DMA((n_seg, n_ctx)),
                pltpu.SemaphoreType.DMA((n_seg, n_ctx)),
                pltpu.SemaphoreType.DMA((2, shards)),
            ],
            compiler_params=pltpu.CompilerParams(
                collective_id=0, has_side_effects=True, vmem_limit_bytes=63 * 1024 * 1024
            ),
        )(*operands)

    return jax.shard_map(
        local,
        mesh=mesh,
        in_specs=(
            P(("groups", "ctx"), "head"),
            P(("groups", "seg", "ctx"), None),
            P(("groups", "seg", "ctx"), None),
            P("groups"),
            P("groups", None),
            P("groups", None),
        ),
        out_specs=P(("groups", "ctx"), "head"),
        check_vma=False,
    )
```

```python
import functools
import math

import jax
import jax.numpy as jnp
import numpy as np
from jax import lax
from jax.experimental import pallas as pl
from jax.experimental.pallas import tpu as pltpu
from jax.sharding import PartitionSpec as P

HEAD_DIM = 128
BLOCK = 64
ROPE_THETA = 500000.0
ROPE_FACTOR = 8.0
LOW_FACTOR = 1.0
HIGH_FACTOR = 4.0
TRAINED_CONTEXT = 8192.0
MASKED = -1e30
EXP2_SCALE = HEAD_DIM ** -0.5 * math.log2(math.e)
MESH = pl.DeviceIdType.MESH


def rope_tables(positions):
    half = HEAD_DIM // 2
    base = ROPE_THETA ** -(np.arange(half, dtype=np.float64) * 2.0 / HEAD_DIM)
    wavelength = 2.0 * np.pi / base
    smooth = (TRAINED_CONTEXT / wavelength - LOW_FACTOR) / (HIGH_FACTOR - LOW_FACTOR)
    blended = (1.0 - smooth) * base / ROPE_FACTOR + smooth * base
    frequency = np.where(
        wavelength < TRAINED_CONTEXT / HIGH_FACTOR,
        base,
        np.where(wavelength > TRAINED_CONTEXT / LOW_FACTOR, base / ROPE_FACTOR, blended),
    )
    angles = positions.astype(np.float64)[:, None] * frequency[None, :]
    cosine = np.concatenate([np.cos(angles), np.cos(angles)], axis=1)
    sine = np.concatenate([-np.sin(angles), np.sin(angles)], axis=1)
    return cosine.astype(np.float32), sine.astype(np.float32)


def flip(index, step, size):
    result, bit = 0, 1
    while bit < size:
        result = result + ((index // bit) % 2 + (step // bit) % 2) % 2 * bit
        bit *= 2
    return result


def kernel(
    n_seg, n_ctx,
    offsets_hbm, q_hbm, k_hbm, v_hbm, vert_hbm, slash_hbm, table_hbm, start_hbm,
    out_ref,
    offsets_ref, q_ref, k_ref, vert_ref, slash_ref, table_ref, start_ref,
    kv, qt, bias_tab, peak, total, numer, held,
    load, send_z, send_x, send_sib, recv,
):
    seg, ctx, head = lax.axis_index("seg"), lax.axis_index("ctx"), lax.axis_index("head")
    rows, heads = q_ref.shape[0], q_ref.shape[1] // HEAD_DIM
    keys = k_ref.shape[0]
    prefix = keys * n_seg * n_ctx - rows * n_ctx
    other = 1 - head
    own = seg * n_ctx + ctx

    def shard(t, u):
        return flip(seg, t, n_seg) * n_ctx + flip(ctx, u, n_ctx)

    loads = [
        pltpu.make_async_copy(source, target, load.at[i])
        for i, (source, target) in enumerate((
            (offsets_hbm, offsets_ref),
            (start_hbm, start_ref),
            (k_hbm, k_ref),
            (table_hbm, table_ref),
            (v_hbm, kv.at[1, own]),
            (q_hbm, q_ref),
            (vert_hbm, vert_ref),
            (slash_hbm, slash_ref),
        ))
    ]
    for copy in loads:
        copy.start()

    barrier = pltpu.get_barrier_semaphore()
    for t in range(1, n_seg):
        pl.semaphore_signal(
            barrier, inc=1, device_id={"seg": flip(seg, t, n_seg)}, device_id_type=MESH
        )
    for u in range(1, n_ctx):
        pl.semaphore_signal(
            barrier, inc=1, device_id={"ctx": flip(ctx, u, n_ctx)}, device_id_type=MESH
        )
    pl.semaphore_signal(barrier, inc=1, device_id={"head": other}, device_id_type=MESH)

    def rotation(index):
        ocos = start_ref[0, pl.ds(index, 1), :]
        osin = start_ref[1, pl.ds(index, 1), :]
        cosine = ocos * table_ref[0] - osin * table_ref[1]
        sine = osin * table_ref[0] + ocos * table_ref[1]
        return cosine, sine

    def rotate(x, cosine, sine):
        x = x.astype(jnp.float32)
        return x * cosine + pltpu.roll(x, HEAD_DIM // 2, 1) * sine

    for copy in loads[:4]:
        copy.wait()
    cosine, sine = rotation(offsets_ref[own] // keys)
    kv[0, own] = rotate(k_ref[...], cosine, sine).astype(jnp.bfloat16)
    loads[4].wait()

    pl.semaphore_wait(barrier, n_seg + n_ctx - 1)

    def copy_z(t):
        return pltpu.make_async_remote_copy(
            src_ref=kv.at[head, own], dst_ref=kv.at[head, own],
            send_sem=send_z.at[t], recv_sem=recv.at[head, own],
            device_id={"seg": flip(seg, t, n_seg)}, device_id_type=MESH,
        )

    def copy_x(t, u):
        index = shard(t, 0)
        return pltpu.make_async_remote_copy(
            src_ref=kv.at[head, index], dst_ref=kv.at[head, index],
            send_sem=send_x.at[t, u], recv_sem=recv.at[head, index],
            device_id={"ctx": flip(ctx, u, n_ctx)}, device_id_type=MESH,
        )

    def copy_sib(t, u):
        index = shard(t, u)
        return pltpu.make_async_remote_copy(
            src_ref=kv.at[head, index], dst_ref=kv.at[head, index],
            send_sem=send_sib.at[t, u], recv_sem=recv.at[head, index],
            device_id={"head": other}, device_id_type=MESH,
        )

    def arrived(kind, index):
        pltpu.make_async_remote_copy(
            src_ref=kv.at[kind, index], dst_ref=kv.at[kind, index],
            send_sem=send_z.at[0], recv_sem=recv.at[kind, index],
            device_id={"head": other}, device_id_type=MESH,
        ).wait_recv()

    for u in range(1, n_ctx):
        copy_x(0, u).start()
    for t in range(1, n_seg):
        copy_z(t).start()

    for copy in loads[5:]:
        copy.wait()
    cosine, sine = rotation((prefix + ctx * rows) // keys)
    for h in range(heads):
        x = q_ref[:, h * HEAD_DIM : (h + 1) * HEAD_DIM]
        qt[:, h * rows : (h + 1) * rows] = rotate(x, cosine, sine).T.astype(jnp.bfloat16)

    lists, blocks = vert_ref.shape[0], bias_tab.shape[0]
    block_id = lax.broadcasted_iota(jnp.int32, (lists, blocks), 1)
    from_slash = (
        prefix // BLOCK + lax.broadcasted_iota(jnp.int32, slash_ref.shape, 0) - slash_ref[...]
    )
    vertical = vert_ref[...]
    hit = vertical[:, 0:1] == block_id
    for i in range(1, vertical.shape[1]):
        hit = hit | (vertical[:, i : i + 1] == block_id)
    for i in range(from_slash.shape[1]):
        hit = hit | (from_slash[:, i : i + 1] == block_id)
    list_id = lax.broadcasted_iota(jnp.int32, (lists, rows), 0)
    token_list = ctx * (rows // BLOCK) + lax.broadcasted_iota(jnp.int32, (lists, rows), 1) // BLOCK
    pick = jnp.where(list_id == token_list, 1.0, 0.0)
    spread = lax.dot_general(
        jnp.where(hit, 1.0, 0.0).T, pick, (((1,), (0,)), ((), ())),
        preferred_element_type=jnp.float32,
    )
    bias_tab[...] = jnp.where(spread > 0.5, 0.0, MASKED)

    lead = (
        prefix + ctx * rows
        + lax.broadcasted_iota(jnp.int32, (BLOCK, rows), 1)
        - lax.broadcasted_iota(jnp.int32, (BLOCK, rows), 0)
    )

    def attend(index, first=False):
        offset = offsets_ref[index]
        pieces = []
        for i in range(keys // BLOCK):
            row = bias_tab[pl.ds(offset // BLOCK + i, 1), :]
            pieces.append(jnp.where(lead >= offset + i * BLOCK, row, MASKED))
        bias = jnp.concatenate(pieces, axis=0)
        key_tile = kv[0, index]
        value_tile = kv[1, index].T
        spans = [slice(h * rows, (h + 1) * rows) for h in range(heads)]
        fresh, old = [], []
        for columns in spans:
            scores = (
                jnp.dot(key_tile, qt[:, columns], preferred_element_type=jnp.float32) + bias
            )
            held[:, columns] = scores
            fresh.append(jnp.max(scores, axis=0, keepdims=True))
        if not first:
            old = [peak[:, columns] for columns in spans]
            fresh = [jnp.maximum(a, b) for a, b in zip(old, fresh)]
        for h, columns in enumerate(spans):
            weights = jnp.exp2((held[:, columns] - fresh[h]) * EXP2_SCALE)
            added = jnp.sum(weights, axis=0, keepdims=True)
            product = jnp.dot(
                value_tile, weights.astype(jnp.bfloat16), preferred_element_type=jnp.float32
            )
            if not first:
                rescale = jnp.exp2((old[h] - fresh[h]) * EXP2_SCALE)
                added = added + total[:, columns] * rescale
                product = product + numer[:, columns] * rescale
            total[:, columns] = added
            numer[:, columns] = product
        for h, columns in enumerate(spans):
            peak[:, columns] = fresh[h]

    attend(own, True)

    def across(t):
        for u in range(1, n_ctx):
            arrived(head, shard(t, u))
            copy_sib(t, u).start()

    def attend_across(t):
        for u in range(1, n_ctx):
            arrived(other, shard(t, u))
            attend(shard(t, u))

    def step(t, carry):
        arrived(head, shard(t, 0))
        for u in range(1, n_ctx):
            copy_x(t, u).start()
        copy_sib(t, 0).start()
        across(t - 1)
        attend_across(t - 1)
        arrived(other, shard(t, 0))
        attend(shard(t, 0))
        return carry

    lax.fori_loop(1, n_seg, step, 0)
    across(n_seg - 1)
    attend_across(n_seg - 1)

    for h in range(heads):
        columns = slice(h * rows, (h + 1) * rows)
        out_ref[:, h * HEAD_DIM : (h + 1) * HEAD_DIM] = (
            (numer[:, columns] / total[:, columns]).T.astype(jnp.bfloat16)
        )

    for t in range(1, n_seg):
        copy_z(t).wait_send()
        copy_sib(t, 0).wait_send()
    for t in range(n_seg):
        for u in range(1, n_ctx):
            copy_x(t, u).wait_send()
            copy_sib(t, u).wait_send()


def solution(mesh):
    n_seg, n_ctx = mesh.shape["seg"], mesh.shape["ctx"]

    def local(queries, cached_keys, cached_values, key_offsets, vertical_blocks, slash_offsets):
        rows, columns = queries.shape
        heads = columns // HEAD_DIM
        keys = cached_keys.shape[0]
        shards = n_seg * n_ctx
        blocks = -(-(keys * shards // BLOCK) // 128) * 128
        table = np.stack(rope_tables(np.arange(keys)))
        start = np.stack(rope_tables(np.arange(shards) * keys))
        operands = (
            key_offsets, queries, cached_keys, cached_values, vertical_blocks, slash_offsets,
            table, start,
        )
        return pl.pallas_call(
            functools.partial(kernel, n_seg, n_ctx),
            out_shape=jax.ShapeDtypeStruct((rows, columns), jnp.bfloat16),
            in_specs=[pl.BlockSpec(memory_space=pltpu.HBM)] * len(operands),
            out_specs=pl.BlockSpec(memory_space=pltpu.VMEM),
            scratch_shapes=[
                pltpu.SMEM(key_offsets.shape, jnp.int32),
                pltpu.VMEM(queries.shape, jnp.bfloat16),
                pltpu.VMEM(cached_keys.shape, jnp.bfloat16),
                pltpu.VMEM(vertical_blocks.shape, jnp.int32),
                pltpu.VMEM(slash_offsets.shape, jnp.int32),
                pltpu.VMEM(table.shape, jnp.float32),
                pltpu.VMEM(start.shape, jnp.float32),
                pltpu.VMEM((2, shards, keys, HEAD_DIM), jnp.bfloat16),
                pltpu.VMEM((HEAD_DIM, heads * rows), jnp.bfloat16),
                pltpu.VMEM((blocks, rows), jnp.float32),
                pltpu.VMEM((1, heads * rows), jnp.float32),
                pltpu.VMEM((1, heads * rows), jnp.float32),
                pltpu.VMEM((HEAD_DIM, heads * rows), jnp.float32),
                pltpu.VMEM((keys, heads * rows), jnp.float32),
                pltpu.SemaphoreType.DMA((len(operands),)),
                pltpu.SemaphoreType.DMA((n_seg,)),
                pltpu.SemaphoreType.DMA((n_seg, n_ctx)),
                pltpu.SemaphoreType.DMA((n_seg, n_ctx)),
                pltpu.SemaphoreType.DMA((2, shards)),
            ],
            compiler_params=pltpu.CompilerParams(
                collective_id=0, has_side_effects=True, vmem_limit_bytes=63 * 1024 * 1024
            ),
        )(*operands)

    return jax.shard_map(
        local,
        mesh=mesh,
        in_specs=(
            P(("groups", "ctx"), "head"),
            P(("groups", "seg", "ctx"), None),
            P(("groups", "seg", "ctx"), None),
            P("groups"),
            P("groups", None),
            P("groups", None),
        ),
        out_specs=P(("groups", "ctx"), "head"),
        check_vma=False,
    )
```

```python
import functools
import math

import jax
import jax.numpy as jnp
import numpy as np
from jax import lax
from jax.experimental import pallas as pl
from jax.experimental.pallas import tpu as pltpu
from jax.sharding import PartitionSpec as P

HEAD_DIM = 128
BLOCK = 64
ROPE_THETA = 500000.0
ROPE_FACTOR = 8.0
LOW_FACTOR = 1.0
HIGH_FACTOR = 4.0
TRAINED_CONTEXT = 8192.0
MASKED = -1e30
EXP2_SCALE = HEAD_DIM ** -0.5 * math.log2(math.e)
MESH = pl.DeviceIdType.MESH


def rope_tables(positions):
    half = HEAD_DIM // 2
    base = ROPE_THETA ** -(np.arange(half, dtype=np.float64) * 2.0 / HEAD_DIM)
    wavelength = 2.0 * np.pi / base
    smooth = (TRAINED_CONTEXT / wavelength - LOW_FACTOR) / (HIGH_FACTOR - LOW_FACTOR)
    blended = (1.0 - smooth) * base / ROPE_FACTOR + smooth * base
    frequency = np.where(
        wavelength < TRAINED_CONTEXT / HIGH_FACTOR,
        base,
        np.where(wavelength > TRAINED_CONTEXT / LOW_FACTOR, base / ROPE_FACTOR, blended),
    )
    angles = positions.astype(np.float64)[:, None] * frequency[None, :]
    cosine = np.concatenate([np.cos(angles), np.cos(angles)], axis=1)
    sine = np.concatenate([-np.sin(angles), np.sin(angles)], axis=1)
    return cosine.astype(np.float32), sine.astype(np.float32)


def flip(index, step, size):
    result, bit = 0, 1
    while bit < size:
        result = result + ((index // bit) % 2 + (step // bit) % 2) % 2 * bit
        bit *= 2
    return result


def kernel(
    n_seg, n_ctx,
    offsets_hbm, q_hbm, k_hbm, v_hbm, vert_hbm, slash_hbm, table_hbm, start_hbm,
    out_ref,
    offsets_ref, q_ref, k_ref, vert_ref, slash_ref, table_ref, start_ref,
    kv, qt, bias_tab, peak, total, numer, held,
    load, send_z, send_x, send_sib, recv,
):
    seg, ctx, head = lax.axis_index("seg"), lax.axis_index("ctx"), lax.axis_index("head")
    rows, heads = q_ref.shape[0], q_ref.shape[1] // HEAD_DIM
    keys = k_ref.shape[0]
    prefix = keys * n_seg * n_ctx - rows * n_ctx
    other = 1 - head
    own = seg * n_ctx + ctx

    def shard(t, u):
        return flip(seg, t, n_seg) * n_ctx + flip(ctx, u, n_ctx)

    loads = [
        pltpu.make_async_copy(source, target, load.at[i])
        for i, (source, target) in enumerate((
            (offsets_hbm, offsets_ref),
            (start_hbm, start_ref),
            (k_hbm, k_ref),
            (table_hbm, table_ref),
            (v_hbm, kv.at[1, own]),
            (q_hbm, q_ref),
            (vert_hbm, vert_ref),
            (slash_hbm, slash_ref),
        ))
    ]
    for copy in loads:
        copy.start()

    barrier = pltpu.get_barrier_semaphore()
    for t in range(1, n_seg):
        pl.semaphore_signal(
            barrier, inc=1, device_id={"seg": flip(seg, t, n_seg)}, device_id_type=MESH
        )
    for u in range(1, n_ctx):
        pl.semaphore_signal(
            barrier, inc=1, device_id={"ctx": flip(ctx, u, n_ctx)}, device_id_type=MESH
        )
    pl.semaphore_signal(barrier, inc=1, device_id={"head": other}, device_id_type=MESH)

    def rotation(index):
        ocos = start_ref[0, pl.ds(index, 1), :]
        osin = start_ref[1, pl.ds(index, 1), :]
        cosine = ocos * table_ref[0] - osin * table_ref[1]
        sine = osin * table_ref[0] + ocos * table_ref[1]
        return cosine, sine

    def rotate(x, cosine, sine):
        x = x.astype(jnp.float32)
        return x * cosine + pltpu.roll(x, HEAD_DIM // 2, 1) * sine

    for copy in loads[:4]:
        copy.wait()
    cosine, sine = rotation(offsets_ref[own] // keys)
    kv[0, own] = rotate(k_ref[...], cosine, sine).astype(jnp.bfloat16)
    loads[4].wait()

    pl.semaphore_wait(barrier, n_seg + n_ctx - 1)

    def copy_z(t):
        return pltpu.make_async_remote_copy(
            src_ref=kv.at[head, own], dst_ref=kv.at[head, own],
            send_sem=send_z.at[t], recv_sem=recv.at[head, own],
            device_id={"seg": flip(seg, t, n_seg)}, device_id_type=MESH,
        )

    def copy_x(t, u):
        index = shard(t, 0)
        return pltpu.make_async_remote_copy(
            src_ref=kv.at[head, index], dst_ref=kv.at[head, index],
            send_sem=send_x.at[t, u], recv_sem=recv.at[head, index],
            device_id={"ctx": flip(ctx, u, n_ctx)}, device_id_type=MESH,
        )

    def copy_sib(t, u):
        index = shard(t, u)
        return pltpu.make_async_remote_copy(
            src_ref=kv.at[head, index], dst_ref=kv.at[head, index],
            send_sem=send_sib.at[t, u], recv_sem=recv.at[head, index],
            device_id={"head": other}, device_id_type=MESH,
        )

    def arrived(kind, index):
        pltpu.make_async_remote_copy(
            src_ref=kv.at[kind, index], dst_ref=kv.at[kind, index],
            send_sem=send_z.at[0], recv_sem=recv.at[kind, index],
            device_id={"head": other}, device_id_type=MESH,
        ).wait_recv()

    for t in range(1, n_seg):
        copy_z(t).start()
    for u in range(1, n_ctx):
        copy_x(0, u).start()

    for copy in loads[5:]:
        copy.wait()
    cosine, sine = rotation((prefix + ctx * rows) // keys)
    for h in range(heads):
        x = q_ref[:, h * HEAD_DIM : (h + 1) * HEAD_DIM]
        qt[:, h * rows : (h + 1) * rows] = rotate(x, cosine, sine).T.astype(jnp.bfloat16)

    lists, blocks = vert_ref.shape[0], bias_tab.shape[0]
    block_id = lax.broadcasted_iota(jnp.int32, (lists, blocks), 1)
    from_slash = (
        prefix // BLOCK + lax.broadcasted_iota(jnp.int32, slash_ref.shape, 0) - slash_ref[...]
    )
    vertical = vert_ref[...]
    hit = vertical[:, 0:1] == block_id
    for i in range(1, vertical.shape[1]):
        hit = hit | (vertical[:, i : i + 1] == block_id)
    for i in range(from_slash.shape[1]):
        hit = hit | (from_slash[:, i : i + 1] == block_id)
    list_id = lax.broadcasted_iota(jnp.int32, (lists, rows), 0)
    token_list = ctx * (rows // BLOCK) + lax.broadcasted_iota(jnp.int32, (lists, rows), 1) // BLOCK
    pick = jnp.where(list_id == token_list, 1.0, 0.0)
    spread = lax.dot_general(
        jnp.where(hit, 1.0, 0.0).T, pick, (((1,), (0,)), ((), ())),
        preferred_element_type=jnp.float32,
    )
    bias_tab[...] = jnp.where(spread > 0.5, 0.0, MASKED)

    lead = (
        prefix + ctx * rows
        + lax.broadcasted_iota(jnp.int32, (BLOCK, rows), 1)
        - lax.broadcasted_iota(jnp.int32, (BLOCK, rows), 0)
    )

    def attend(index, first=False):
        offset = offsets_ref[index]
        pieces = []
        for i in range(keys // BLOCK):
            row = bias_tab[pl.ds(offset // BLOCK + i, 1), :]
            pieces.append(jnp.where(lead >= offset + i * BLOCK, row, MASKED))
        bias = jnp.concatenate(pieces, axis=0)
        key_tile = kv[0, index]
        value_tile = kv[1, index].T
        spans = [slice(h * rows, (h + 1) * rows) for h in range(heads)]
        fresh, old = [], []
        for columns in spans:
            scores = (
                jnp.dot(key_tile, qt[:, columns], preferred_element_type=jnp.float32) + bias
            )
            held[:, columns] = scores
            fresh.append(jnp.max(scores, axis=0, keepdims=True))
        if not first:
            old = [peak[:, columns] for columns in spans]
            fresh = [jnp.maximum(a, b) for a, b in zip(old, fresh)]
        for h, columns in enumerate(spans):
            weights = jnp.exp2((held[:, columns] - fresh[h]) * EXP2_SCALE)
            added = jnp.sum(weights, axis=0, keepdims=True)
            product = jnp.dot(
                value_tile, weights.astype(jnp.bfloat16), preferred_element_type=jnp.float32
            )
            if not first:
                rescale = jnp.exp2((old[h] - fresh[h]) * EXP2_SCALE)
                added = added + total[:, columns] * rescale
                product = product + numer[:, columns] * rescale
            total[:, columns] = added
            numer[:, columns] = product
        for h, columns in enumerate(spans):
            peak[:, columns] = fresh[h]

    attend(own, True)

    def across(t):
        for u in range(1, n_ctx):
            arrived(head, shard(t, u))
            copy_sib(t, u).start()

    def attend_across(t):
        for u in range(1, n_ctx):
            arrived(other, shard(t, u))
            attend(shard(t, u))

    def forward(t):
        arrived(head, shard(t, 0))
        for u in range(1, n_ctx):
            copy_x(t, u).start()
        copy_sib(t, 0).start()
        across(t - 1)

    def attend_along(t):
        arrived(other, shard(t, 0))
        attend(shard(t, 0))

    def step(t, carry):
        forward(t)
        attend_along(t - 1)
        attend_across(t - 2)
        return carry

    forward(1)
    lax.fori_loop(2, n_seg, step, 0)
    attend_across(n_seg - 2)
    across(n_seg - 1)
    attend_along(n_seg - 1)
    attend_across(n_seg - 1)

    for h in range(heads):
        columns = slice(h * rows, (h + 1) * rows)
        out_ref[:, h * HEAD_DIM : (h + 1) * HEAD_DIM] = (
            (numer[:, columns] / total[:, columns]).T.astype(jnp.bfloat16)
        )

    for t in range(1, n_seg):
        copy_z(t).wait_send()
        copy_sib(t, 0).wait_send()
    for t in range(n_seg):
        for u in range(1, n_ctx):
            copy_x(t, u).wait_send()
            copy_sib(t, u).wait_send()


def solution(mesh):
    n_seg, n_ctx = mesh.shape["seg"], mesh.shape["ctx"]

    def local(queries, cached_keys, cached_values, key_offsets, vertical_blocks, slash_offsets):
        rows, columns = queries.shape
        heads = columns // HEAD_DIM
        keys = cached_keys.shape[0]
        shards = n_seg * n_ctx
        blocks = -(-(keys * shards // BLOCK) // 128) * 128
        table = np.stack(rope_tables(np.arange(keys)))
        start = np.stack(rope_tables(np.arange(shards) * keys))
        operands = (
            key_offsets, queries, cached_keys, cached_values, vertical_blocks, slash_offsets,
            table, start,
        )
        return pl.pallas_call(
            functools.partial(kernel, n_seg, n_ctx),
            out_shape=jax.ShapeDtypeStruct((rows, columns), jnp.bfloat16),
            in_specs=[pl.BlockSpec(memory_space=pltpu.HBM)] * len(operands),
            out_specs=pl.BlockSpec(memory_space=pltpu.VMEM),
            scratch_shapes=[
                pltpu.SMEM(key_offsets.shape, jnp.int32),
                pltpu.VMEM(queries.shape, jnp.bfloat16),
                pltpu.VMEM(cached_keys.shape, jnp.bfloat16),
                pltpu.VMEM(vertical_blocks.shape, jnp.int32),
                pltpu.VMEM(slash_offsets.shape, jnp.int32),
                pltpu.VMEM(table.shape, jnp.float32),
                pltpu.VMEM(start.shape, jnp.float32),
                pltpu.VMEM((2, shards, keys, HEAD_DIM), jnp.bfloat16),
                pltpu.VMEM((HEAD_DIM, heads * rows), jnp.bfloat16),
                pltpu.VMEM((blocks, rows), jnp.float32),
                pltpu.VMEM((1, heads * rows), jnp.float32),
                pltpu.VMEM((1, heads * rows), jnp.float32),
                pltpu.VMEM((HEAD_DIM, heads * rows), jnp.float32),
                pltpu.VMEM((keys, heads * rows), jnp.float32),
                pltpu.SemaphoreType.DMA((len(operands),)),
                pltpu.SemaphoreType.DMA((n_seg,)),
                pltpu.SemaphoreType.DMA((n_seg, n_ctx)),
                pltpu.SemaphoreType.DMA((n_seg, n_ctx)),
                pltpu.SemaphoreType.DMA((2, shards)),
            ],
            compiler_params=pltpu.CompilerParams(
                collective_id=0, has_side_effects=True, vmem_limit_bytes=63 * 1024 * 1024
            ),
        )(*operands)

    return jax.shard_map(
        local,
        mesh=mesh,
        in_specs=(
            P(("groups", "ctx"), "head"),
            P(("groups", "seg", "ctx"), None),
            P(("groups", "seg", "ctx"), None),
            P("groups"),
            P("groups", None),
            P("groups", None),
        ),
        out_specs=P(("groups", "ctx"), "head"),
        check_vma=False,
    )
```

```python
import functools
import math

import jax
import jax.numpy as jnp
import numpy as np
from jax import lax
from jax.experimental import pallas as pl
from jax.experimental.pallas import tpu as pltpu
from jax.sharding import PartitionSpec as P

HEAD_DIM = 128
BLOCK = 64
ROPE_THETA = 500000.0
ROPE_FACTOR = 8.0
LOW_FACTOR = 1.0
HIGH_FACTOR = 4.0
TRAINED_CONTEXT = 8192.0
MASKED = -1e30
EXP2_SCALE = HEAD_DIM ** -0.5 * math.log2(math.e)
MESH = pl.DeviceIdType.MESH


def rope_tables(positions):
    half = HEAD_DIM // 2
    base = ROPE_THETA ** -(np.arange(half, dtype=np.float64) * 2.0 / HEAD_DIM)
    wavelength = 2.0 * np.pi / base
    smooth = (TRAINED_CONTEXT / wavelength - LOW_FACTOR) / (HIGH_FACTOR - LOW_FACTOR)
    blended = (1.0 - smooth) * base / ROPE_FACTOR + smooth * base
    frequency = np.where(
        wavelength < TRAINED_CONTEXT / HIGH_FACTOR,
        base,
        np.where(wavelength > TRAINED_CONTEXT / LOW_FACTOR, base / ROPE_FACTOR, blended),
    )
    angles = positions.astype(np.float64)[:, None] * frequency[None, :]
    cosine = np.concatenate([np.cos(angles), np.cos(angles)], axis=1)
    sine = np.concatenate([-np.sin(angles), np.sin(angles)], axis=1)
    return cosine.astype(np.float32), sine.astype(np.float32)


def flip(index, step, size):
    result, bit = 0, 1
    while bit < size:
        result = result + ((index // bit) % 2 + (step // bit) % 2) % 2 * bit
        bit *= 2
    return result


def kernel(
    n_seg, n_ctx,
    offsets_hbm, q_hbm, k_hbm, v_hbm, vert_hbm, slash_hbm, table_hbm, start_hbm,
    out_ref,
    offsets_ref, q_ref, k_ref, vert_ref, slash_ref, table_ref, start_ref,
    kv, qt, bias_tab, peak, total, numer, held,
    load, send_z, send_x, send_sib, recv,
):
    seg, ctx, head = lax.axis_index("seg"), lax.axis_index("ctx"), lax.axis_index("head")
    rows, heads = q_ref.shape[0], q_ref.shape[1] // HEAD_DIM
    keys = k_ref.shape[0]
    prefix = keys * n_seg * n_ctx - rows * n_ctx
    other = 1 - head
    own = seg * n_ctx + ctx

    def shard(t, u):
        return flip(seg, t, n_seg) * n_ctx + flip(ctx, u, n_ctx)

    loads = [
        pltpu.make_async_copy(source, target, load.at[i])
        for i, (source, target) in enumerate((
            (offsets_hbm, offsets_ref),
            (start_hbm, start_ref),
            (k_hbm, k_ref),
            (table_hbm, table_ref),
            (v_hbm, kv.at[1, own]),
            (q_hbm, q_ref),
            (vert_hbm, vert_ref),
            (slash_hbm, slash_ref),
        ))
    ]
    for copy in loads:
        copy.start()

    barrier = pltpu.get_barrier_semaphore()
    for t in range(1, n_seg):
        pl.semaphore_signal(
            barrier, inc=1, device_id={"seg": flip(seg, t, n_seg)}, device_id_type=MESH
        )
    for u in range(1, n_ctx):
        pl.semaphore_signal(
            barrier, inc=1, device_id={"ctx": flip(ctx, u, n_ctx)}, device_id_type=MESH
        )
    pl.semaphore_signal(barrier, inc=1, device_id={"head": other}, device_id_type=MESH)

    def rotation(index):
        ocos = start_ref[0, pl.ds(index, 1), :]
        osin = start_ref[1, pl.ds(index, 1), :]
        cosine = ocos * table_ref[0] - osin * table_ref[1]
        sine = osin * table_ref[0] + ocos * table_ref[1]
        return cosine, sine

    def rotate(x, cosine, sine):
        x = x.astype(jnp.float32)
        return x * cosine + pltpu.roll(x, HEAD_DIM // 2, 1) * sine

    for copy in loads[:4]:
        copy.wait()
    cosine, sine = rotation(offsets_ref[own] // keys)
    kv[0, own] = rotate(k_ref[...], cosine, sine).astype(jnp.bfloat16)
    loads[4].wait()

    pl.semaphore_wait(barrier, n_seg + n_ctx - 1)

    def copy_z(t):
        return pltpu.make_async_remote_copy(
            src_ref=kv.at[head, own], dst_ref=kv.at[head, own],
            send_sem=send_z.at[t], recv_sem=recv.at[head, own],
            device_id={"seg": flip(seg, t, n_seg)}, device_id_type=MESH,
        )

    def copy_x(t, u):
        index = shard(t, 0)
        return pltpu.make_async_remote_copy(
            src_ref=kv.at[head, index], dst_ref=kv.at[head, index],
            send_sem=send_x.at[t, u], recv_sem=recv.at[head, index],
            device_id={"ctx": flip(ctx, u, n_ctx)}, device_id_type=MESH,
        )

    def copy_sib(t, u):
        index = shard(t, u)
        return pltpu.make_async_remote_copy(
            src_ref=kv.at[head, index], dst_ref=kv.at[head, index],
            send_sem=send_sib.at[t, u], recv_sem=recv.at[head, index],
            device_id={"head": other}, device_id_type=MESH,
        )

    def arrived(kind, index):
        pltpu.make_async_remote_copy(
            src_ref=kv.at[kind, index], dst_ref=kv.at[kind, index],
            send_sem=send_z.at[0], recv_sem=recv.at[kind, index],
            device_id={"head": other}, device_id_type=MESH,
        ).wait_recv()

    for t in range(1, n_seg):
        copy_z(t).start()
    for u in range(1, n_ctx):
        copy_x(0, u).start()

    for copy in loads[5:]:
        copy.wait()
    cosine, sine = rotation((prefix + ctx * rows) // keys)
    for h in range(heads):
        x = q_ref[:, h * HEAD_DIM : (h + 1) * HEAD_DIM]
        qt[:, h * rows : (h + 1) * rows] = rotate(x, cosine, sine).T.astype(jnp.bfloat16)

    lists, blocks = vert_ref.shape[0], bias_tab.shape[0]
    block_id = lax.broadcasted_iota(jnp.int32, (lists, blocks), 1)
    from_slash = (
        prefix // BLOCK + lax.broadcasted_iota(jnp.int32, slash_ref.shape, 0) - slash_ref[...]
    )
    vertical = vert_ref[...]
    hit = vertical[:, 0:1] == block_id
    for i in range(1, vertical.shape[1]):
        hit = hit | (vertical[:, i : i + 1] == block_id)
    for i in range(from_slash.shape[1]):
        hit = hit | (from_slash[:, i : i + 1] == block_id)
    list_id = lax.broadcasted_iota(jnp.int32, (lists, rows), 0)
    token_list = ctx * (rows // BLOCK) + lax.broadcasted_iota(jnp.int32, (lists, rows), 1) // BLOCK
    pick = jnp.where(list_id == token_list, 1.0, 0.0)
    spread = lax.dot_general(
        jnp.where(hit, 1.0, 0.0).T, pick, (((1,), (0,)), ((), ())),
        preferred_element_type=jnp.float32,
    )
    bias_tab[...] = jnp.where(spread > 0.5, 0.0, MASKED)

    lead = (
        prefix + ctx * rows
        + lax.broadcasted_iota(jnp.int32, (BLOCK, rows), 1)
        - lax.broadcasted_iota(jnp.int32, (BLOCK, rows), 0)
    )

    def attend(index, first=False):
        offset = offsets_ref[index]
        pieces = []
        for i in range(keys // BLOCK):
            row = bias_tab[pl.ds(offset // BLOCK + i, 1), :]
            pieces.append(jnp.where(lead >= offset + i * BLOCK, row, MASKED))
        bias = jnp.concatenate(pieces, axis=0)
        key_tile = kv[0, index]
        value_tile = kv[1, index].T
        spans = [slice(h * rows, (h + 1) * rows) for h in range(heads)]
        fresh, old = [], []
        for columns in spans:
            scores = (
                jnp.dot(key_tile, qt[:, columns], preferred_element_type=jnp.float32) + bias
            )
            held[:, columns] = scores
            fresh.append(jnp.max(scores, axis=0, keepdims=True))
        if not first:
            old = [peak[:, columns] for columns in spans]
            fresh = [jnp.maximum(a, b) for a, b in zip(old, fresh)]
        for h, columns in enumerate(spans):
            weights = jnp.exp2((held[:, columns] - fresh[h]) * EXP2_SCALE)
            added = jnp.sum(weights, axis=0, keepdims=True)
            product = jnp.dot(
                value_tile, weights.astype(jnp.bfloat16), preferred_element_type=jnp.float32
            )
            if not first:
                rescale = jnp.exp2((old[h] - fresh[h]) * EXP2_SCALE)
                added = added + total[:, columns] * rescale
                product = product + numer[:, columns] * rescale
            total[:, columns] = added
            numer[:, columns] = product
        for h, columns in enumerate(spans):
            peak[:, columns] = fresh[h]

    attend(own, True)

    def across(t):
        for u in range(1, n_ctx):
            arrived(head, shard(t, u))
            copy_sib(t, u).start()

    def attend_across(t):
        for u in range(1, n_ctx):
            arrived(other, shard(t, u))
            attend(shard(t, u))

    def forward(t):
        arrived(head, shard(t, 0))
        for u in range(1, n_ctx):
            copy_x(t, u).start()
        copy_sib(t, 0).start()
        across(t - 1)

    def attend_along(t):
        arrived(other, shard(t, 0))
        attend(shard(t, 0))

    def step(t, carry):
        forward(t)
        attend_along(t - 1)
        attend_across(t - 2)
        return carry

    forward(1)
    lax.fori_loop(2, n_seg, step, 0)
    attend_across(n_seg - 2)
    across(n_seg - 1)
    attend_along(n_seg - 1)
    attend_across(n_seg - 1)

    for h in range(heads):
        columns = slice(h * rows, (h + 1) * rows)
        out_ref[:, h * HEAD_DIM : (h + 1) * HEAD_DIM] = (
            (numer[:, columns] / total[:, columns]).T.astype(jnp.bfloat16)
        )

    for t in range(1, n_seg):
        copy_z(t).wait_send()
        copy_sib(t, 0).wait_send()
    for t in range(n_seg):
        for u in range(1, n_ctx):
            copy_x(t, u).wait_send()
            copy_sib(t, u).wait_send()


def solution(mesh):
    n_seg, n_ctx = mesh.shape["seg"], mesh.shape["ctx"]

    def local(queries, cached_keys, cached_values, key_offsets, vertical_blocks, slash_offsets):
        rows, columns = queries.shape
        heads = columns // HEAD_DIM
        keys = cached_keys.shape[0]
        shards = n_seg * n_ctx
        blocks = -(-(keys * shards // BLOCK) // 128) * 128
        table = np.stack(rope_tables(np.arange(keys)))
        start = np.stack(rope_tables(np.arange(shards) * keys))
        operands = (
            key_offsets, queries, cached_keys, cached_values, vertical_blocks, slash_offsets,
            table, start,
        )
        return pl.pallas_call(
            functools.partial(kernel, n_seg, n_ctx),
            out_shape=jax.ShapeDtypeStruct((rows, columns), jnp.bfloat16),
            in_specs=[pl.BlockSpec(memory_space=pltpu.HBM)] * len(operands),
            out_specs=pl.BlockSpec(memory_space=pltpu.VMEM),
            scratch_shapes=[
                pltpu.SMEM(key_offsets.shape, jnp.int32),
                pltpu.VMEM(queries.shape, jnp.bfloat16),
                pltpu.VMEM(cached_keys.shape, jnp.bfloat16),
                pltpu.VMEM(vertical_blocks.shape, jnp.int32),
                pltpu.VMEM(slash_offsets.shape, jnp.int32),
                pltpu.VMEM(table.shape, jnp.float32),
                pltpu.VMEM(start.shape, jnp.float32),
                pltpu.VMEM((2, shards, keys, HEAD_DIM), jnp.bfloat16),
                pltpu.VMEM((HEAD_DIM, heads * rows), jnp.bfloat16),
                pltpu.VMEM((blocks, rows), jnp.float32),
                pltpu.VMEM((1, heads * rows), jnp.float32),
                pltpu.VMEM((1, heads * rows), jnp.float32),
                pltpu.VMEM((HEAD_DIM, heads * rows), jnp.float32),
                pltpu.VMEM((keys, heads * rows), jnp.float32),
                pltpu.SemaphoreType.DMA((len(operands),)),
                pltpu.SemaphoreType.DMA((n_seg,)),
                pltpu.SemaphoreType.DMA((n_seg, n_ctx)),
                pltpu.SemaphoreType.DMA((n_seg, n_ctx)),
                pltpu.SemaphoreType.DMA((2, shards)),
            ],
            compiler_params=pltpu.CompilerParams(
                collective_id=0, has_side_effects=True, vmem_limit_bytes=48 * 1024 * 1024
            ),
        )(*(pltpu.with_memory_space_constraint(x, pltpu.HBM) for x in map(jnp.asarray, operands)))

    return jax.shard_map(
        local,
        mesh=mesh,
        in_specs=(
            P(("groups", "ctx"), "head"),
            P(("groups", "seg", "ctx"), None),
            P(("groups", "seg", "ctx"), None),
            P("groups"),
            P("groups", None),
            P("groups", None),
        ),
        out_specs=P(("groups", "ctx"), "head"),
        check_vma=False,
    )
```

```python
import functools
import math

import jax
import jax.numpy as jnp
import numpy as np
from jax import lax
from jax.experimental import pallas as pl
from jax.experimental.pallas import tpu as pltpu
from jax.sharding import PartitionSpec as P

HEAD_DIM = 128
BLOCK = 64
ROPE_THETA = 500000.0
ROPE_FACTOR = 8.0
LOW_FACTOR = 1.0
HIGH_FACTOR = 4.0
TRAINED_CONTEXT = 8192.0
MASKED = -1e30
PIECES = 2
EXP2_SCALE = HEAD_DIM ** -0.5 * math.log2(math.e)
MESH = pl.DeviceIdType.MESH


def rope_tables(positions):
    half = HEAD_DIM // 2
    base = ROPE_THETA ** -(np.arange(half, dtype=np.float64) * 2.0 / HEAD_DIM)
    wavelength = 2.0 * np.pi / base
    smooth = (TRAINED_CONTEXT / wavelength - LOW_FACTOR) / (HIGH_FACTOR - LOW_FACTOR)
    blended = (1.0 - smooth) * base / ROPE_FACTOR + smooth * base
    frequency = np.where(
        wavelength < TRAINED_CONTEXT / HIGH_FACTOR,
        base,
        np.where(wavelength > TRAINED_CONTEXT / LOW_FACTOR, base / ROPE_FACTOR, blended),
    )
    angles = positions.astype(np.float64)[:, None] * frequency[None, :]
    cosine = np.concatenate([np.cos(angles), np.cos(angles)], axis=1)
    sine = np.concatenate([-np.sin(angles), np.sin(angles)], axis=1)
    return cosine.astype(np.float32), sine.astype(np.float32)


def flip(index, step, size):
    result, bit = 0, 1
    while bit < size:
        result = result + ((index // bit) % 2 + (step // bit) % 2) % 2 * bit
        bit *= 2
    return result


def kernel(
    n_seg, n_ctx,
    offsets_hbm, q_hbm, k_hbm, v_hbm, vert_hbm, slash_hbm, table_hbm, start_hbm,
    out_ref,
    offsets_ref, q_ref, k_ref, vert_ref, slash_ref, table_ref, start_ref,
    kv, qt, bias_tab, peak, total, numer, held,
    load, send_z, send_x, send_sib, recv,
):
    seg, ctx, head = lax.axis_index("seg"), lax.axis_index("ctx"), lax.axis_index("head")
    rows, heads = q_ref.shape[0], q_ref.shape[1] // HEAD_DIM
    keys = k_ref.shape[0]
    prefix = keys * n_seg * n_ctx - rows * n_ctx
    other = 1 - head
    own = seg * n_ctx + ctx

    def shard(t, u):
        return flip(seg, t, n_seg) * n_ctx + flip(ctx, u, n_ctx)

    loads = [
        pltpu.make_async_copy(source, target, load.at[i])
        for i, (source, target) in enumerate((
            (offsets_hbm, offsets_ref),
            (start_hbm, start_ref),
            (k_hbm, k_ref),
            (table_hbm, table_ref),
            (v_hbm, kv.at[1, own]),
            (q_hbm, q_ref),
            (vert_hbm, vert_ref),
            (slash_hbm, slash_ref),
        ))
    ]
    for copy in loads:
        copy.start()

    barrier = pltpu.get_barrier_semaphore()
    for t in range(1, n_seg):
        pl.semaphore_signal(
            barrier, inc=1, device_id={"seg": flip(seg, t, n_seg)}, device_id_type=MESH
        )
    for u in range(1, n_ctx):
        pl.semaphore_signal(
            barrier, inc=1, device_id={"ctx": flip(ctx, u, n_ctx)}, device_id_type=MESH
        )
    pl.semaphore_signal(barrier, inc=1, device_id={"head": other}, device_id_type=MESH)

    def rotation(index):
        ocos = start_ref[0, pl.ds(index, 1), :]
        osin = start_ref[1, pl.ds(index, 1), :]
        cosine = ocos * table_ref[0] - osin * table_ref[1]
        sine = osin * table_ref[0] + ocos * table_ref[1]
        return cosine, sine

    def rotate(x, cosine, sine):
        x = x.astype(jnp.float32)
        return x * cosine + pltpu.roll(x, HEAD_DIM // 2, 1) * sine

    for copy in loads[:4]:
        copy.wait()
    cosine, sine = rotation(offsets_ref[own] // keys)
    kv[0, own] = rotate(k_ref[...], cosine, sine).astype(jnp.bfloat16)
    loads[4].wait()

    pl.semaphore_wait(barrier, n_seg + n_ctx - 1)

    def piece(kind, index, p):
        return kv.at[kind, index, pl.ds(p * (keys // PIECES), keys // PIECES)]

    def copy_z(t, p):
        return pltpu.make_async_remote_copy(
            src_ref=piece(head, own, p), dst_ref=piece(head, own, p),
            send_sem=send_z.at[t, p], recv_sem=recv.at[head, own, p],
            device_id={"seg": flip(seg, t, n_seg)}, device_id_type=MESH,
        )

    def copy_x(t, u, p):
        index = shard(t, 0)
        return pltpu.make_async_remote_copy(
            src_ref=piece(head, index, p), dst_ref=piece(head, index, p),
            send_sem=send_x.at[t, u, p], recv_sem=recv.at[head, index, p],
            device_id={"ctx": flip(ctx, u, n_ctx)}, device_id_type=MESH,
        )

    def copy_sib(t, u, p):
        index = shard(t, u)
        return pltpu.make_async_remote_copy(
            src_ref=piece(head, index, p), dst_ref=piece(head, index, p),
            send_sem=send_sib.at[t, u, p], recv_sem=recv.at[head, index, p],
            device_id={"head": other}, device_id_type=MESH,
        )

    def arrived(kind, index, p):
        pltpu.make_async_remote_copy(
            src_ref=piece(kind, index, p), dst_ref=piece(kind, index, p),
            send_sem=send_z.at[0, p], recv_sem=recv.at[kind, index, p],
            device_id={"head": other}, device_id_type=MESH,
        ).wait_recv()

    for t in range(1, n_seg):
        for p in range(PIECES):
            copy_z(t, p).start()
    for u in range(1, n_ctx):
        for p in range(PIECES):
            copy_x(0, u, p).start()

    for copy in loads[5:]:
        copy.wait()
    cosine, sine = rotation((prefix + ctx * rows) // keys)
    for h in range(heads):
        x = q_ref[:, h * HEAD_DIM : (h + 1) * HEAD_DIM]
        qt[:, h * rows : (h + 1) * rows] = rotate(x, cosine, sine).T.astype(jnp.bfloat16)

    lists, blocks = vert_ref.shape[0], bias_tab.shape[0]
    block_id = lax.broadcasted_iota(jnp.int32, (lists, blocks), 1)
    from_slash = (
        prefix // BLOCK + lax.broadcasted_iota(jnp.int32, slash_ref.shape, 0) - slash_ref[...]
    )
    vertical = vert_ref[...]
    hit = vertical[:, 0:1] == block_id
    for i in range(1, vertical.shape[1]):
        hit = hit | (vertical[:, i : i + 1] == block_id)
    for i in range(from_slash.shape[1]):
        hit = hit | (from_slash[:, i : i + 1] == block_id)
    list_id = lax.broadcasted_iota(jnp.int32, (lists, rows), 0)
    token_list = ctx * (rows // BLOCK) + lax.broadcasted_iota(jnp.int32, (lists, rows), 1) // BLOCK
    pick = jnp.where(list_id == token_list, 1.0, 0.0)
    spread = lax.dot_general(
        jnp.where(hit, 1.0, 0.0).T, pick, (((1,), (0,)), ((), ())),
        preferred_element_type=jnp.float32,
    )
    bias_tab[...] = jnp.where(spread > 0.5, 0.0, MASKED)

    lead = (
        prefix + ctx * rows
        + lax.broadcasted_iota(jnp.int32, (BLOCK, rows), 1)
        - lax.broadcasted_iota(jnp.int32, (BLOCK, rows), 0)
    )

    def attend(index, first=False):
        offset = offsets_ref[index]
        pieces = []
        for i in range(keys // BLOCK):
            row = bias_tab[pl.ds(offset // BLOCK + i, 1), :]
            pieces.append(jnp.where(lead >= offset + i * BLOCK, row, MASKED))
        bias = jnp.concatenate(pieces, axis=0)
        key_tile = kv[0, index]
        value_tile = kv[1, index].T
        spans = [slice(h * rows, (h + 1) * rows) for h in range(heads)]
        fresh, old = [], []
        for columns in spans:
            scores = (
                jnp.dot(key_tile, qt[:, columns], preferred_element_type=jnp.float32) + bias
            )
            held[:, columns] = scores
            fresh.append(jnp.max(scores, axis=0, keepdims=True))
        if not first:
            old = [peak[:, columns] for columns in spans]
            fresh = [jnp.maximum(a, b) for a, b in zip(old, fresh)]
        for h, columns in enumerate(spans):
            weights = jnp.exp2((held[:, columns] - fresh[h]) * EXP2_SCALE)
            added = jnp.sum(weights, axis=0, keepdims=True)
            product = jnp.dot(
                value_tile, weights.astype(jnp.bfloat16), preferred_element_type=jnp.float32
            )
            if not first:
                rescale = jnp.exp2((old[h] - fresh[h]) * EXP2_SCALE)
                added = added + total[:, columns] * rescale
                product = product + numer[:, columns] * rescale
            total[:, columns] = added
            numer[:, columns] = product
        for h, columns in enumerate(spans):
            peak[:, columns] = fresh[h]

    attend(own, True)

    def across(t):
        for u in range(1, n_ctx):
            for p in range(PIECES):
                arrived(head, shard(t, u), p)
                copy_sib(t, u, p).start()

    def attend_across(t):
        for u in range(1, n_ctx):
            for p in range(PIECES):
                arrived(other, shard(t, u), p)
            attend(shard(t, u))

    def forward(t):
        for p in range(PIECES):
            arrived(head, shard(t, 0), p)
            for u in range(1, n_ctx):
                copy_x(t, u, p).start()
            copy_sib(t, 0, p).start()
        across(t - 1)

    def attend_along(t):
        for p in range(PIECES):
            arrived(other, shard(t, 0), p)
        attend(shard(t, 0))

    def step(t, carry):
        forward(t)
        attend_along(t - 1)
        attend_across(t - 2)
        return carry

    forward(1)
    lax.fori_loop(2, n_seg, step, 0)
    attend_across(n_seg - 2)
    across(n_seg - 1)
    attend_along(n_seg - 1)
    attend_across(n_seg - 1)

    for h in range(heads):
        columns = slice(h * rows, (h + 1) * rows)
        out_ref[:, h * HEAD_DIM : (h + 1) * HEAD_DIM] = (
            (numer[:, columns] / total[:, columns]).T.astype(jnp.bfloat16)
        )

    for p in range(PIECES):
        for t in range(1, n_seg):
            copy_z(t, p).wait_send()
            copy_sib(t, 0, p).wait_send()
        for t in range(n_seg):
            for u in range(1, n_ctx):
                copy_x(t, u, p).wait_send()
                copy_sib(t, u, p).wait_send()


def solution(mesh):
    n_seg, n_ctx = mesh.shape["seg"], mesh.shape["ctx"]

    def local(queries, cached_keys, cached_values, key_offsets, vertical_blocks, slash_offsets):
        rows, columns = queries.shape
        heads = columns // HEAD_DIM
        keys = cached_keys.shape[0]
        shards = n_seg * n_ctx
        blocks = -(-(keys * shards // BLOCK) // 128) * 128
        table = np.stack(rope_tables(np.arange(keys)))
        start = np.stack(rope_tables(np.arange(shards) * keys))
        operands = (
            key_offsets, queries, cached_keys, cached_values, vertical_blocks, slash_offsets,
            table, start,
        )
        return pl.pallas_call(
            functools.partial(kernel, n_seg, n_ctx),
            out_shape=jax.ShapeDtypeStruct((rows, columns), jnp.bfloat16),
            in_specs=[pl.BlockSpec(memory_space=pltpu.HBM)] * len(operands),
            out_specs=pl.BlockSpec(memory_space=pltpu.VMEM),
            scratch_shapes=[
                pltpu.SMEM(key_offsets.shape, jnp.int32),
                pltpu.VMEM(queries.shape, jnp.bfloat16),
                pltpu.VMEM(cached_keys.shape, jnp.bfloat16),
                pltpu.VMEM(vertical_blocks.shape, jnp.int32),
                pltpu.VMEM(slash_offsets.shape, jnp.int32),
                pltpu.VMEM(table.shape, jnp.float32),
                pltpu.VMEM(start.shape, jnp.float32),
                pltpu.VMEM((2, shards, keys, HEAD_DIM), jnp.bfloat16),
                pltpu.VMEM((HEAD_DIM, heads * rows), jnp.bfloat16),
                pltpu.VMEM((blocks, rows), jnp.float32),
                pltpu.VMEM((1, heads * rows), jnp.float32),
                pltpu.VMEM((1, heads * rows), jnp.float32),
                pltpu.VMEM((HEAD_DIM, heads * rows), jnp.float32),
                pltpu.VMEM((keys, heads * rows), jnp.float32),
                pltpu.SemaphoreType.DMA((len(operands),)),
                pltpu.SemaphoreType.DMA((n_seg, PIECES)),
                pltpu.SemaphoreType.DMA((n_seg, n_ctx, PIECES)),
                pltpu.SemaphoreType.DMA((n_seg, n_ctx, PIECES)),
                pltpu.SemaphoreType.DMA((2, shards, PIECES)),
            ],
            compiler_params=pltpu.CompilerParams(
                collective_id=0, has_side_effects=True, vmem_limit_bytes=48 * 1024 * 1024
            ),
        )(*(pltpu.with_memory_space_constraint(x, pltpu.HBM) for x in map(jnp.asarray, operands)))

    return jax.shard_map(
        local,
        mesh=mesh,
        in_specs=(
            P(("groups", "ctx"), "head"),
            P(("groups", "seg", "ctx"), None),
            P(("groups", "seg", "ctx"), None),
            P("groups"),
            P("groups", None),
            P("groups", None),
        ),
        out_specs=P(("groups", "ctx"), "head"),
        check_vma=False,
    )
```
